32 devices in a mesh: cluster: 4 (over y, x), sub: 8 (over z, core).
Axes of the slice: x: 2, y: 2, z: 4, core: 2. Of those that a mesh axis runs over, the one named last changes fastest.
Arguments:
- factor_tiles: float32 [32, 300, 128, 128], P(('cluster', 'sub')), may hold values from -1 to 2, as said below
- rigid_modes: float32 [32, 6, 3072], P(('cluster', 'sub')), may hold values from -6 to 6
- load_cases: float32 [32, 32, 3072], P(('cluster', 'sub')), may hold values from -6 to 6
- coarse_load: float32 [24, 32], replicated, may hold values from -5120 to 5120
- peer_slots: int32 [32, 32, 96], P(('cluster', 'sub')), may hold values from 0 to 640, as said below
- slot_unknown: int32 [32, 640], P(('cluster', 'sub')), may hold values from 0 to 3072, as said below
Outputs:
- multipliers: float32 [32, 640, 32], P(('cluster', 'sub'))
- projected: float32 [32, 640, 32], P(('cluster', 'sub'))
The draws below stay inside these ranges and needn't reach their ends.
Inputs may be any that keep to these rules, and one draw needn't show every extreme that they name: For k below the number of multipliers shared by subdomains a and b, peer_slots[a, b, k] is the slot of a holding the k-th of them, in the same order as peer_slots[b, a, k]; other places hold 640; each slot is listed at most once in peer_slots[a]; a shares multipliers only with the subdomain of the same index within the next or previous cluster (at most 96) and with subdomains of its own cluster whose grid positions differ from its own by at most one in each coordinate, where index w within a cluster stands at z = w // (8 / 2), x = (w % (8 / 2)) // 2, y = w % 2; such a pair shares at most 96 multipliers if the positions differ in one coordinate, at most 12 if in two, at most 3 if in three; some pair shares exactly 96, some pair differing in two coordinates exactly 12. `slot_unknown`: distinct over the listed slots of one subdomain; exactly 3072 on the slots that peer_slots[s] does not list, and every subdomain has such slots. `factor_tiles`: tiles with I = J are lower triangular with diagonal entries from 1 to 2.
All inputs are finite; a program needn't handle non-finite values.
Results may differ from the reference program's by a relative error of at most 0.0003.
Values sent between devices are 32-bit elements; how exact they have to be, the bound alone decides.
A program may use at most 320 MiB of HBM per device.

```python
import math
import jax
import jax.numpy as jnp
import numpy as np
from jax import lax

UNKNOWNS = 3072
SLOTS = 640
TILE = 128
MODES = 6
PAIR_MOST = 96
LOADS = 32
ITERS = 2
TILE_ROWS = 24
TILES = 300
SUBS = 32
COARSE = 24
N_CLUSTER = 4
N_SUB = 8


def cluster_geometry():
    breadth_y = 2 + 2 * min(1, N_SUB // 32)
    half_count = N_SUB // 2
    device_ids = np.arange(SUBS)
    cluster_of = device_ids // N_SUB
    within = device_ids % N_SUB
    breadth_x = half_count // breadth_y
    coord_z = within // half_count
    coord_y = within % breadth_y
    coord_x = within % half_count // breadth_y
    delta_x = np.abs(coord_x[:, None] - coord_x[None, :])
    delta_y = np.abs(coord_y[:, None] - coord_y[None, :])
    delta_z = np.abs(coord_z[:, None] - coord_z[None, :])
    same = cluster_of[:, None] == cluster_of[None, :]
    nearby = same & (delta_x <= 1) & (delta_y <= 1) & (delta_z <= 1)
    kinds = np.where(nearby, delta_x + delta_y + delta_z, 0)
    boundary = np.where(cluster_of % 2 == 0, breadth_x - 1, 0)
    crossing = (cluster_of[None, :] == cluster_of[:, None] + 1) & (within[:, None] == within[None, :]) & (coord_x[:, None] == boundary[:, None])
    crossing = crossing | crossing.T
    return np.where(crossing, 1, kinds).astype(np.int32)


def node_pick(subkey):
    return jax.random.permutation(subkey, UNKNOWNS)[:SLOTS]


def draw_topology(key):
    kinds = jnp.asarray(cluster_geometry())
    breadth_y = 2 + 2 * min(1, N_SUB // 32)
    edge_most = 3 * max(2, PAIR_MOST // 24)
    face_key, edge_key, node_key = jax.random.split(jax.random.fold_in(key, 7), 3)
    upper = jnp.asarray(np.triu(np.ones((SUBS, SUBS), bool), 1))
    face = 3 * jax.random.randint(face_key, (SUBS, SUBS), PAIR_MOST // 6, PAIR_MOST // 3 + 1)
    face = jnp.where(upper, face, face.T)
    edge = 3 * jax.random.randint(edge_key, (SUBS, SUBS), 1, max(2, PAIR_MOST // 24) + 1)
    edge = jnp.where(upper, edge, edge.T)
    counts = jnp.where(kinds == 1, face, jnp.where(kinds == 2, edge, jnp.where(kinds == 3, 3, 0)))
    counts = counts.at[0, 1].set(PAIR_MOST).at[1, 0].set(PAIR_MOST)
    counts = counts.at[0, breadth_y + 1].set(edge_most).at[breadth_y + 1, 0].set(edge_most)
    offsets = jnp.cumsum(counts, axis=1) - counts
    places = jnp.arange(PAIR_MOST, dtype=jnp.int32)
    table = jnp.where(places[None, None, :] < counts[:, :, None], offsets[:, :, None] + places[None, None, :], SLOTS)
    totals = jnp.sum(counts, axis=1)
    picks = jax.vmap(node_pick)(jax.random.split(node_key, SUBS))
    nodes = jnp.where(jnp.arange(SLOTS)[None, :] < totals[:, None], picks, UNKNOWNS)
    return (table.astype(jnp.int32), nodes.astype(jnp.int32))


def draw_peer_slots(key, part):
    return draw_topology(key)[0]


def draw_slot_unknown(key, part):
    return draw_topology(key)[1]


def draw_factor_tiles(key, part):
    diagonal_flags = np.zeros(TILES, bool)
    for tile_row in range(TILE_ROWS):
        diagonal_flags[tile_row * (tile_row + 1) // 2 + tile_row] = True
    noise_key, scale_key = jax.random.split(key)
    shape = (SUBS, TILES, TILE, TILE)
    noise = jax.random.normal(noise_key, shape, jnp.float32)
    noise = noise * (0.3 / math.sqrt(UNKNOWNS))
    diagonal = jnp.exp(jax.random.uniform(scale_key, (SUBS, TILES, TILE), jnp.float32, 0.0, math.log(2.0)))
    lower = jnp.asarray(np.tril(np.ones((TILE, TILE), np.float32), -1))
    identity = jnp.asarray(np.eye(TILE, dtype=np.float32))
    diagonal_tiles = noise * lower + identity * diagonal[:, :, None, :]
    return jnp.where(jnp.asarray(diagonal_flags)[None, :, None, None], diagonal_tiles, noise)


def block_levels(own_key, shape, shards, least, high):
    level = 1.0
    for position, blocks in shards:
        draws = jax.random.uniform(jax.random.fold_in(jax.random.fold_in(own_key, 6), position), (blocks,), jnp.float32, least / len(shards), high / len(shards))
        level = level * jnp.repeat(jnp.exp(draws), shape[position] // blocks).reshape((-1,) + (1,) * (len(shape) - 1 - position))
    return level


def bell_draw(rng, extent, scale, bound, cuts=(), held_as=jnp.bfloat16):
    loudness = block_levels(rng, extent, cuts, -0.22, 0.18) if cuts else 1.0
    drawn = jax.random.normal(rng, extent, jnp.float32) * scale * loudness
    return jnp.minimum(jnp.maximum(drawn, -bound), bound).astype(held_as)


def setup_inputs(seed: int = 0) -> dict:
    key_of = jax.random.split(jax.random.key(seed), 7)
    return {
        "factor_tiles": draw_factor_tiles(jax.random.fold_in(key_of[6], 71), 0),
        "rigid_modes": bell_draw(key_of[1], (SUBS, MODES, UNKNOWNS), 1.0, 6.0, ((0, 32),), jnp.float32),
        "load_cases": bell_draw(key_of[2], (SUBS, LOADS, UNKNOWNS), 1.0, 6.0, ((0, 32),), jnp.float32),
        "coarse_load": bell_draw(key_of[3], (COARSE, LOADS), (100 * N_SUB), 5120.0, (), jnp.float32),
        "peer_slots": draw_peer_slots(jax.random.fold_in(key_of[6], 71), 0),
        "slot_unknown": draw_slot_unknown(jax.random.fold_in(key_of[6], 71), 0),
    }


HIGH = lax.Precision.HIGHEST

def unpack(tiles):
    count = tiles.shape[0]
    tile_edge = tiles.shape[1]
    blocks = (math.isqrt(8 * count + 1) - 1) // 2
    stacked = []
    for tile_row in range(blocks):
        pieces = [tiles[tile_row * (tile_row + 1) // 2 + tile_col] for tile_col in range(tile_row + 1)]
        if tile_row + 1 < blocks:
            pieces.append(jnp.zeros((tile_edge, tile_edge * (blocks - tile_row - 1)), tiles.dtype))
        stacked.append(jnp.concatenate(pieces, axis=1))
    return jnp.concatenate(stacked, axis=0)

def local_setup(tiles, rigid_rows, forces, slot_nodes, slot_signs, membership):
    factor = unpack(tiles)
    unknowns = factor.shape[0]
    slot_count = slot_nodes.shape[0]
    gluing = (jnp.arange(unknowns, dtype=jnp.int32)[:, None] == slot_nodes[None, :]).astype(jnp.float32) * slot_signs[None, :]
    solved = jax.scipy.linalg.solve_triangular(factor, jnp.concatenate([gluing, forces.T], axis=1), lower=True)
    spread = solved[:, :slot_count]
    settled = solved[:, slot_count:]
    dual_matrix = jnp.dot(spread.T.astype(jnp.float32), spread.astype(jnp.float32), precision=HIGH, preferred_element_type=jnp.float32)
    dual_load = jnp.dot(spread.T.astype(jnp.float32), settled.astype(jnp.float32), precision=HIGH, preferred_element_type=jnp.float32)
    local_modes = jnp.dot(gluing.T.astype(jnp.float32), rigid_rows.T.astype(jnp.float32), precision=HIGH, preferred_element_type=jnp.float32)
    half_modes = (local_modes[:, None, :] * membership[None, :, None]).reshape(slot_count, -1)
    return (dual_matrix, dual_load, half_modes)

def reference(factor_tiles, rigid_modes, load_cases, coarse_load, peer_slots, slot_unknown):
    subdomains = peer_slots.shape[0]
    peer_order = jnp.arange(subdomains, dtype=jnp.int32)
    upward = jnp.where(peer_order[None, :] > peer_order[:, None], 1.0, -1.0).astype(jnp.float32)
    slot_signs = jnp.zeros((subdomains, SLOTS + 1), jnp.float32).at[peer_order[:, None, None], peer_slots].add(jnp.broadcast_to(upward[:, :, None], peer_slots.shape))[:, :SLOTS]
    membership = (peer_order[:, None] // N_SUB == jnp.arange(N_CLUSTER, dtype=jnp.int32)[None, :]).astype(jnp.float32)

    def setup_one(arrays):
        return local_setup(*arrays)
    dual_matrix, dual_load, half_modes = lax.map(setup_one, (factor_tiles, rigid_modes, load_cases, slot_unknown, slot_signs, membership))

    def pair(values):
        breadth = values.shape[2]
        extended = jnp.concatenate([values, jnp.zeros((subdomains, 1, breadth), values.dtype)], axis=1)

        def incoming(target):
            sources = lax.dynamic_index_in_dim(peer_slots, target, 1, keepdims=False)
            received = extended[peer_order[:, None], sources]
            own_slots = lax.dynamic_index_in_dim(peer_slots, target, 0, keepdims=False)
            summed = jnp.zeros((SLOTS + 1, breadth), values.dtype).at[own_slots.reshape(-1)].add(received.reshape(-1, breadth))
            return summed[:SLOTS]
        return values + lax.map(incoming, peer_order)
    modes = pair(half_modes)
    coarse_gram = 0.5 * jnp.einsum('sjc,sjd->cd', modes, modes, precision=HIGH)
    coarse_factor = jnp.linalg.cholesky(coarse_gram)

    def project(values):
        coarse = 0.5 * jnp.einsum('sjc,sjl->cl', modes, values, precision=HIGH)
        weights = jax.scipy.linalg.cho_solve((coarse_factor, True), coarse)
        return values - jnp.einsum('sjc,cl->sjl', modes, weights, precision=HIGH)

    def apply_dual(values):
        return jnp.einsum('sij,sjl->sil', dual_matrix, values, precision=HIGH)
    start_weights = jax.scipy.linalg.cho_solve((coarse_factor, True), coarse_load)
    multipliers = jnp.einsum('sjc,cl->sjl', modes, start_weights, precision=HIGH)
    residual = pair(dual_load - apply_dual(multipliers))
    projected = project(residual)
    current = 0.5 * lax.optimization_barrier(jnp.sum(projected * projected, axis=(0, 1)))
    direction = projected
    for iteration in range(ITERS):
        image = pair(apply_dual(direction))
        alpha = current / (0.5 * lax.optimization_barrier(jnp.sum(direction * image, axis=(0, 1))))
        multipliers = multipliers + alpha * direction
        residual = residual - alpha * image
        projected = project(residual)
        following = 0.5 * lax.optimization_barrier(jnp.sum(projected * projected, axis=(0, 1)))
        direction = projected + following / current * direction
        current = following
    return (multipliers, projected)
```

```python
import functools

import jax
import jax.numpy as jnp
from jax import lax
from jax.experimental import pallas as pl
from jax.experimental.pallas import tpu as pltpu
from jax.sharding import PartitionSpec as P

ITERS = 2
HIGH = lax.Precision.HIGHEST
BF = jnp.bfloat16
F32 = jnp.float32
EDGE = 128
BLOCK = 256
SMALL = 32
NN = (((1,), (0,)), ((), ()))
NT = (((1,), (1,)), ((), ()))


def split(value):
    high = value.astype(BF)
    return high, (value - high.astype(F32)).astype(BF)


def mul(left, right, dims):
    return lax.dot_general(left, right, dims, preferred_element_type=F32)


def mul3(left, right, dims):
    return mul(left[0], right[0], dims) + (mul(left[1], right[0], dims) + mul(left[0], right[1], dims))


def exact(left, right, dims):
    return lax.dot_general(left, right, dims, precision=HIGH, preferred_element_type=F32)


def invert_tiles(tiles):
    count = len(tiles)
    lane = lax.broadcasted_iota(jnp.int32, (SMALL, EDGE), 1)
    row = lax.broadcasted_iota(jnp.int32, (SMALL, EDGE), 0)
    packed = []
    for tile in tiles:
        total = jnp.zeros((SMALL, EDGE), F32)
        for b in range(EDGE // SMALL):
            total = jnp.where(lane // SMALL == b, tile[b * SMALL : (b + 1) * SMALL], total)
        packed.append(total)
    solved = [jnp.where(lane % SMALL == row, 1.0, 0.0).astype(F32)] * count
    base = lane // SMALL * SMALL
    for k in range(SMALL):
        for t in range(count):
            column = jnp.take_along_axis(packed[t], base + k, axis=1)
            pivot_row = solved[t][k : k + 1] / column[k : k + 1]
            lowered = solved[t] - jnp.where(row > k, column, 0.0) * pivot_row
            solved[t] = jnp.where(row == k, pivot_row, lowered)
    full_row = lax.broadcasted_iota(jnp.int32, (EDGE, EDGE), 0)
    full_col = lax.broadcasted_iota(jnp.int32, (EDGE, EDGE), 1)
    results = []
    for t in range(count):
        results.append(
            jnp.concatenate(
                [jnp.where(lane // SMALL == b, solved[t], 0.0) for b in range(EDGE // SMALL)],
                axis=0,
            )
        )
    size = SMALL
    while size < EDGE:
        below = (full_row // size == full_col // size + 1) & (full_row // size % 2 == 1)
        for t in range(count):
            corner = split(jnp.where(below, tiles[t], 0.0))
            parts = split(results[t])
            first = split(mul3(parts, corner, NN))
            results[t] = results[t] - mul3(first, parts, NN)
        size *= 2
    return results


def solve_kernel(blocks, slots, tiles, nodes, signs, loads, rigid, out, modes, inv_hi, inv_lo, y_hi, y_lo, acc):
    def tile_at(i, j):
        return i * (i + 1) // 2 + j

    group = 2

    def invert(step, carry):
        picks = [step * group + g for g in range(group)]
        diagonals = []
        for i in picks:
            diagonals.append(tiles[tile_at(2 * i, 2 * i)])
            diagonals.append(tiles[tile_at(2 * i + 1, 2 * i + 1)])
        inverses = invert_tiles(diagonals)
        for g, i in enumerate(picks):
            upper, lower = inverses[2 * g], inverses[2 * g + 1]
            corner = split(tiles[tile_at(2 * i + 1, 2 * i)])
            below = -mul3(split(mul3(split(lower), corner, NN)), split(upper), NN)
            whole = jnp.concatenate(
                [
                    jnp.concatenate([upper, jnp.zeros((EDGE, EDGE), F32)], axis=1),
                    jnp.concatenate([below, lower], axis=1),
                ],
                axis=0,
            )
            inv_hi[i], inv_lo[i] = split(whole)
        return carry

    lax.fori_loop(0, blocks // group, invert, 0)
    out[...] = jnp.zeros_like(out)
    modes[...] = jnp.zeros_like(modes)

    def block_row(i, carry):
        columns = pl.ds(pl.multiple_of(i * BLOCK, BLOCK), BLOCK)
        place = i * BLOCK + lax.broadcasted_iota(jnp.int32, (slots, BLOCK), 1)
        gluing = jnp.where(place == nodes[...], signs[...], 0.0)
        modes[...] += exact(rigid[:, columns], gluing, NT)
        acc[:slots] = gluing
        acc[slots:] = loads[:, columns]

        def subtract(j, inner):
            above, under = tile_at(2 * i, 2 * j), tile_at(2 * i + 1, 2 * j)
            block = jnp.concatenate(
                [
                    jnp.concatenate([tiles[above], tiles[above + 1]], axis=1),
                    jnp.concatenate([tiles[under], tiles[under + 1]], axis=1),
                ],
                axis=0,
            )
            acc[...] -= mul3((y_hi[j], y_lo[j]), split(block), NT)
            return inner

        lax.fori_loop(0, i, subtract, 0)
        y = split(mul3(split(acc[...]), (inv_hi[i], inv_lo[i]), NT))
        y_hi[i], y_lo[i] = y
        out[...] += mul3(y, (y[0][:slots], y[1][:slots]), NT)
        return carry

    lax.fori_loop(0, blocks, block_row, 0)


def solve(tiles, nodes, signs, loads, rigid):
    slots = nodes.shape[0]
    unknowns = loads.shape[1]
    wide = slots + loads.shape[0]
    blocks = unknowns // BLOCK
    vmem = pl.BlockSpec(memory_space=pltpu.VMEM)
    return pl.pallas_call(
        functools.partial(solve_kernel, blocks, slots),
        out_shape=(
            jax.ShapeDtypeStruct((wide, slots), F32),
            jax.ShapeDtypeStruct((rigid.shape[0], slots), F32),
        ),
        in_specs=[vmem] * 5,
        out_specs=(vmem, vmem),
        scratch_shapes=[
            pltpu.VMEM((blocks, BLOCK, BLOCK), BF),
            pltpu.VMEM((blocks, BLOCK, BLOCK), BF),
            pltpu.VMEM((blocks, wide, BLOCK), BF),
            pltpu.VMEM((blocks, wide, BLOCK), BF),
            pltpu.VMEM((wide, BLOCK), F32),
        ],
        compiler_params=pltpu.CompilerParams(vmem_limit_bytes=56 * 1024 * 1024),
    )(tiles, nodes, signs, loads, rigid)


def local(factor_tiles, rigid_modes, load_cases, coarse_load, peer_slots, slot_unknown):
    sub_count = lax.axis_size("sub")
    cluster_count = lax.axis_size("cluster")
    cluster_index = lax.axis_index("cluster")
    own_index = cluster_index * sub_count + lax.axis_index("sub")
    table = peer_slots[0]
    devices, most = table.shape
    slots = slot_unknown.shape[1]
    mode_count = rigid_modes.shape[1]

    lower_peer = own_index - sub_count
    upper_peer = own_index + sub_count
    lower_slots = jnp.where(lower_peer >= 0, table[jnp.maximum(lower_peer, 0)], slots)
    upper_slots = jnp.where(upper_peer < devices, table[jnp.minimum(upper_peer, devices - 1)], slots)
    inner_slots = lax.dynamic_slice_in_dim(table, cluster_index * sub_count, sub_count, 0)
    lists = jnp.concatenate([inner_slots, lower_slots[None], upper_slots[None]], axis=0)
    peers = jnp.concatenate(
        [cluster_index * sub_count + jnp.arange(sub_count, dtype=jnp.int32), lower_peer[None], upper_peer[None]]
    )
    upward = jnp.where(peers > own_index, 1.0, -1.0).astype(F32)
    flat = lists.reshape(-1)
    hits = jnp.arange(slots, dtype=jnp.int32)[:, None] == flat[None, :]
    signs = jnp.sum(jnp.where(hits, jnp.repeat(upward, most)[None, :], 0.0), axis=1, keepdims=True)
    select = hits.astype(F32)

    rigid = jnp.pad(rigid_modes[0], ((0, 8 - mode_count), (0, 0)))
    solved, half = solve(factor_tiles[0], slot_unknown[0][:, None], signs, load_cases[0], rigid)
    dual = solved[:slots]
    dual_load = solved[slots:]
    half = half[:mode_count]

    def exchange(values):
        breadth = values.shape[0]
        picked = exact(values, select, NN).reshape(breadth, -1, most)
        received = lax.all_to_all(picked[:, :sub_count], "sub", split_axis=1, concat_axis=1, tiled=True)
        climb = [(i, i + 1) for i in range(cluster_count - 1)]
        from_lower = lax.ppermute(picked[:, sub_count + 1], "cluster", climb)
        from_upper = lax.ppermute(picked[:, sub_count], "cluster", [(b, a) for a, b in climb])
        received = jnp.concatenate([received, from_lower[:, None], from_upper[:, None]], axis=1)
        return values + exact(received.reshape(breadth, -1), select, NT)

    def everywhere(values):
        copies = jnp.broadcast_to(values[None], (devices,) + values.shape)
        return jnp.sum(lax.all_to_all(copies, ("cluster", "sub"), split_axis=0, concat_axis=0, tiled=True), axis=0)

    member = (jnp.arange(cluster_count, dtype=jnp.int32) == cluster_index).astype(F32)
    modes = exchange((half[None] * member[:, None, None]).reshape(-1, slots))
    gram = everywhere(0.5 * exact(modes, modes, NT))
    factor = jnp.linalg.cholesky(gram)
    inverse = jax.scipy.linalg.solve_triangular(factor, jnp.eye(factor.shape[0], dtype=F32), lower=True)

    def coarse_solve(values):
        return exact(exact(values, inverse, NT), inverse, NN)

    def dot(left, right):
        return jnp.sum(left * right, axis=1, keepdims=True)

    multipliers = exact(coarse_solve(coarse_load.T), modes, NN)
    value = dual_load - exact(multipliers, dual, NT)
    coarse = everywhere(exact(value, modes, NT))
    residual = exchange(value)
    projected = residual - exact(coarse_solve(coarse), modes, NN)
    width = modes.shape[0]
    current = direction = image = dual_direction = share = None
    for iteration in range(ITERS):
        applied = exact(projected, dual, NT)
        pieces = [exact(applied, modes, NT), dot(projected, applied), 0.5 * dot(projected, projected)]
        if iteration:
            pieces += [dot(projected, dual_direction), dot(direction, dual_direction)]
        sums = everywhere(jnp.concatenate(pieces, axis=1))
        paired = exchange(applied)
        added = sums[:, :width]
        curved = sums[:, width : width + 1]
        following = sums[:, width + 1 : width + 2]
        if iteration:
            beta = following / current
            curved = curved + beta * (2.0 * sums[:, width + 2 : width + 3] + beta * sums[:, width + 3 : width + 4])
            direction = projected + beta * direction
            image = paired + beta * image
            share = added + beta * share
            dual_direction = applied + beta * dual_direction
        else:
            direction, image, share, dual_direction = projected, paired, added, applied
        current = following
        alpha = current / curved
        multipliers = multipliers + alpha * direction
        residual = residual - alpha * image
        coarse = coarse - alpha * share
        projected = residual - exact(coarse_solve(coarse), modes, NN)
    return (multipliers.T[None], projected.T[None])


def solution(mesh):
    return jax.shard_map(
        local,
        mesh=mesh,
        in_specs=(
            P(("cluster", "sub"), None, None, None),
            P(("cluster", "sub"), None, None),
            P(("cluster", "sub"), None, None),
            P(),
            P(("cluster", "sub"), None, None),
            P(("cluster", "sub"), None),
        ),
        out_specs=(P(("cluster", "sub"), None, None), P(("cluster", "sub"), None, None)),
        check_vma=False,
    )
```

```python
import functools

import jax
import jax.numpy as jnp
from jax import lax
from jax.experimental import pallas as pl
from jax.experimental.pallas import tpu as pltpu
from jax.sharding import PartitionSpec as P

ITERS = 2
HIGH = lax.Precision.HIGHEST
BF = jnp.bfloat16
F32 = jnp.float32
EDGE = 128
BLOCK = 256
SMALL = 32
NN = (((1,), (0,)), ((), ()))
NT = (((1,), (1,)), ((), ()))


def split(value):
    high = value.astype(BF)
    return high, (value - high.astype(F32)).astype(BF)


def mul(left, right, dims):
    return lax.dot_general(left, right, dims, preferred_element_type=F32)


def mul3(left, right, dims):
    return mul(left[0], right[0], dims) + (mul(left[1], right[0], dims) + mul(left[0], right[1], dims))


def exact(left, right, dims):
    return lax.dot_general(left, right, dims, precision=HIGH, preferred_element_type=F32)


def thirds(value):
    high = value.astype(BF).astype(F32)
    rest = value - high
    middle = rest.astype(BF).astype(F32)
    return jnp.concatenate([high, middle, rest - middle], axis=0).astype(BF)


def picked_by(value, ones, dims):
    rows = value.shape[0]
    parts = mul(thirds(value), ones, dims)
    return parts[:rows] + parts[rows : 2 * rows] + parts[2 * rows :]


def invert_tiles(tiles):
    count = len(tiles)
    lane = lax.broadcasted_iota(jnp.int32, (SMALL, EDGE), 1)
    row = lax.broadcasted_iota(jnp.int32, (SMALL, EDGE), 0)
    packed = []
    for tile in tiles:
        total = jnp.zeros((SMALL, EDGE), F32)
        for b in range(EDGE // SMALL):
            total = jnp.where(lane // SMALL == b, tile[b * SMALL : (b + 1) * SMALL], total)
        packed.append(total)
    solved = [jnp.where(lane % SMALL == row, 1.0, 0.0).astype(F32)] * count
    base = lane // SMALL * SMALL
    for k in range(SMALL):
        for t in range(count):
            column = jnp.take_along_axis(packed[t], base + k, axis=1)
            pivot_row = solved[t][k : k + 1] / column[k : k + 1]
            lowered = solved[t] - jnp.where(row > k, column, 0.0) * pivot_row
            solved[t] = jnp.where(row == k, pivot_row, lowered)
    full_row = lax.broadcasted_iota(jnp.int32, (EDGE, EDGE), 0)
    full_col = lax.broadcasted_iota(jnp.int32, (EDGE, EDGE), 1)
    results = []
    for t in range(count):
        results.append(
            jnp.concatenate(
                [jnp.where(lane // SMALL == b, solved[t], 0.0) for b in range(EDGE // SMALL)],
                axis=0,
            )
        )
    size = SMALL
    while size < EDGE:
        below = (full_row // size == full_col // size + 1) & (full_row // size % 2 == 1)
        for t in range(count):
            corner = split(jnp.where(below, tiles[t], 0.0))
            parts = split(results[t])
            first = split(mul3(parts, corner, NN))
            results[t] = results[t] - mul3(first, parts, NN)
        size *= 2
    return results


def solve_kernel(blocks, slots, tiles, nodes, signs, loads, rigid, out, modes, inv_hi, inv_lo, y_hi, y_lo, acc):
    def tile_at(i, j):
        return i * (i + 1) // 2 + j

    group = 2

    def invert(step, carry):
        picks = [step * group + g for g in range(group)]
        diagonals = []
        for i in picks:
            diagonals.append(tiles[tile_at(2 * i, 2 * i)])
            diagonals.append(tiles[tile_at(2 * i + 1, 2 * i + 1)])
        inverses = invert_tiles(diagonals)
        for g, i in enumerate(picks):
            upper, lower = inverses[2 * g], inverses[2 * g + 1]
            corner = split(tiles[tile_at(2 * i + 1, 2 * i)])
            below = -mul3(split(mul3(split(lower), corner, NN)), split(upper), NN)
            whole = jnp.concatenate(
                [
                    jnp.concatenate([upper, jnp.zeros((EDGE, EDGE), F32)], axis=1),
                    jnp.concatenate([below, lower], axis=1),
                ],
                axis=0,
            )
            inv_hi[i], inv_lo[i] = split(whole)
        return carry

    lax.fori_loop(0, blocks // group, invert, 0)
    out[...] = jnp.zeros_like(out)
    modes[...] = jnp.zeros_like(modes)

    def block_row(i, carry):
        columns = pl.ds(pl.multiple_of(i * BLOCK, BLOCK), BLOCK)
        place = i * BLOCK + lax.broadcasted_iota(jnp.int32, (slots, BLOCK), 1)
        gluing = jnp.where(place == nodes[...], signs[...], 0.0)
        modes[...] += mul(thirds(rigid[:, columns]), gluing.astype(BF), NT)
        acc[:slots] = gluing
        acc[slots:] = loads[:, columns]

        def subtract(j, inner):
            above, under = tile_at(2 * i, 2 * j), tile_at(2 * i + 1, 2 * j)
            block = jnp.concatenate(
                [
                    jnp.concatenate([tiles[above], tiles[above + 1]], axis=1),
                    jnp.concatenate([tiles[under], tiles[under + 1]], axis=1),
                ],
                axis=0,
            )
            acc[...] -= mul3((y_hi[j], y_lo[j]), split(block), NT)
            return inner

        lax.fori_loop(0, i, subtract, 0)
        y = split(mul3(split(acc[...]), (inv_hi[i], inv_lo[i]), NT))
        y_hi[i], y_lo[i] = y
        out[...] += mul3(y, (y[0][:slots], y[1][:slots]), NT)
        return carry

    lax.fori_loop(0, blocks, block_row, 0)


def solve(tiles, nodes, signs, loads, rigid):
    slots = nodes.shape[0]
    unknowns = loads.shape[1]
    wide = slots + loads.shape[0]
    blocks = unknowns // BLOCK
    vmem = pl.BlockSpec(memory_space=pltpu.VMEM)
    return pl.pallas_call(
        functools.partial(solve_kernel, blocks, slots),
        out_shape=(
            jax.ShapeDtypeStruct((wide, slots), F32),
            jax.ShapeDtypeStruct((3 * rigid.shape[0], slots), F32),
        ),
        in_specs=[vmem] * 5,
        out_specs=(vmem, vmem),
        scratch_shapes=[
            pltpu.VMEM((blocks, BLOCK, BLOCK), BF),
            pltpu.VMEM((blocks, BLOCK, BLOCK), BF),
            pltpu.VMEM((blocks, wide, BLOCK), BF),
            pltpu.VMEM((blocks, wide, BLOCK), BF),
            pltpu.VMEM((wide, BLOCK), F32),
        ],
        compiler_params=pltpu.CompilerParams(vmem_limit_bytes=56 * 1024 * 1024),
    )(tiles, nodes, signs, loads, rigid)


def cg_kernel(
    clusters, subs, width, solved, half, coarse_load, select, mult_out, proj_out,
    send, recv, cross_send, cross_recv, dual_hi, dual_lo, send_sem, recv_sem, cross_send_sem, cross_recv_sem,
):
    loads, slots = mult_out.shape
    cluster = lax.axis_index("cluster")
    sub = lax.axis_index("sub")
    inner = subs - 1
    blocks = inner + 2
    lower, upper = inner, inner + 1
    started = []
    lane = lax.broadcasted_iota(jnp.int32, (loads, EDGE), 1)

    recv[0, lower] = jnp.zeros(recv.shape[2:], F32)
    recv[0, upper] = jnp.zeros(recv.shape[2:], F32)
    for turn in range(2, 2 + 1 + ITERS):
        recv[turn, lower] = jnp.zeros(recv.shape[2:], F32)
        recv[turn, upper] = jnp.zeros(recv.shape[2:], F32)

    barrier = pltpu.get_barrier_semaphore()
    for step in range(1, subs):
        pl.semaphore_signal(
            barrier, inc=1, device_id=(cluster, lax.rem(sub + step, subs)), device_id_type=pl.DeviceIdType.MESH
        )
    for step in range(1, clusters):
        pl.semaphore_signal(
            barrier, inc=1, device_id=(lax.rem(cluster + step, clusters), sub), device_id_type=pl.DeviceIdType.MESH
        )
    pl.semaphore_wait(barrier, subs - 1 + clusters - 1)

    def to_neighbour(turn, source, target, device):
        return pltpu.make_async_remote_copy(
            src_ref=send.at[turn, source, pl.ds(0, loads)],
            dst_ref=recv.at[turn, target, pl.ds(0, loads)],
            send_sem=send_sem.at[turn, source],
            recv_sem=recv_sem.at[turn, target],
            device_id=(device, sub),
            device_id_type=pl.DeviceIdType.MESH,
        )

    def talk(turn, values, payload):
        first = 0 if values is not None else loads
        last = loads + 8 if payload is not None else loads
        if values is not None:
            chosen = picked_by(values, select[...], NN)
            for b in range(blocks):
                send[turn, b, :loads] = chosen[:, b * EDGE : (b + 1) * EDGE]
        if payload is not None:
            compact = payload[:8]
            for part in range(1, loads // 8):
                compact = compact + pltpu.roll(payload[8 * part : 8 * part + 8], 32 * part, 1)
            for b in range(inner):
                send[turn, b, loads:] = compact
        copies = []
        for step in range(1, subs):
            copies.append(
                pltpu.make_async_remote_copy(
                    src_ref=send.at[turn, step - 1, pl.ds(first, last - first)],
                    dst_ref=recv.at[turn, subs - step - 1, pl.ds(first, last - first)],
                    send_sem=send_sem.at[turn, step - 1],
                    recv_sem=recv_sem.at[turn, subs - step - 1],
                    device_id=(cluster, lax.rem(sub + step, subs)),
                    device_id_type=pl.DeviceIdType.MESH,
                )
            )
            copies[-1].start()
        if values is not None:
            down = to_neighbour(turn, lower, upper, lax.rem(cluster + clusters - 1, clusters))
            up = to_neighbour(turn, upper, lower, lax.rem(cluster + 1, clusters))

            @pl.when(cluster > 0)
            def _():
                down.start()

            @pl.when(cluster < clusters - 1)
            def _():
                up.start()

        for copy in copies:
            copy.wait_recv()
        started.extend(copies)
        total = paired = None
        across = []
        if payload is not None:
            total = compact
            for b in range(inner):
                total = total + recv[turn, b, loads:]
            cross_send[turn] = total
            for step in range(1, clusters):
                across.append(
                    pltpu.make_async_remote_copy(
                        src_ref=cross_send.at[turn],
                        dst_ref=cross_recv.at[turn, clusters - step - 1],
                        send_sem=cross_send_sem.at[turn, step - 1],
                        recv_sem=cross_recv_sem.at[turn, clusters - step - 1],
                        device_id=(lax.rem(cluster + step, clusters), sub),
                        device_id_type=pl.DeviceIdType.MESH,
                    )
                )
                across[-1].start()
        if values is not None:

            @pl.when(cluster > 0)
            def _():
                up.wait_recv()
                down.wait_send()

            @pl.when(cluster < clusters - 1)
            def _():
                down.wait_recv()
                up.wait_send()

            received = jnp.concatenate([recv[turn, b, :loads] for b in range(blocks)], axis=1)
            paired = values + picked_by(received, select[...], NT)
        if payload is not None:
            for copy in across:
                copy.wait_recv()
            started.extend(across)
            for b in range(clusters - 1):
                total = total + cross_recv[turn, b]
            rows = [total] + [pltpu.roll(total, EDGE - 32 * part, 1) for part in range(1, loads // 8)]
            total = jnp.where(lane < 32, jnp.concatenate(rows, axis=0), 0.0)
        return paired, total

    modes, _ = talk(0, half[...], None)
    spread = jnp.concatenate([modes, jnp.zeros((EDGE - loads, slots), F32)], axis=0)
    _, gram = talk(1, None, 0.5 * exact(modes, spread, NT))
    row = lax.broadcasted_iota(jnp.int32, (loads, EDGE), 0)
    inverse = jnp.where(row == lane, 1.0, 0.0).astype(F32)
    for k in range(width):
        scale = 1.0 / jnp.sqrt(gram[k : k + 1, k : k + 1])
        gram_row = gram[k : k + 1] * scale
        inverse_row = inverse[k : k + 1] * scale
        factor = jnp.where(row[:, :1] > k, gram[:, k : k + 1] * scale, 0.0)
        gram = gram - factor * gram_row
        inverse = jnp.where(row == k, inverse_row, inverse - factor * inverse_row)

    def along_modes(values):
        weights = exact(exact(values, inverse, NT), inverse, NN)
        return exact(weights, spread, NN)

    dual_hi[...], dual_lo[...] = split(solved[:slots])

    def apply_dual(values):
        high = values.astype(BF).astype(F32)
        stacked = jnp.concatenate([high, values - high], axis=0).astype(BF)
        product = mul(stacked, dual_lo[...], NT) + mul(stacked, dual_hi[...], NT)
        return product[:loads] + product[loads:]

    def dot(left, right):
        return jnp.sum(left * right, axis=1, keepdims=True)

    multipliers = along_modes(coarse_load[...])
    value = solved[slots:] - apply_dual(multipliers)
    residual, coarse = talk(2, value, exact(value, spread, NT))
    coarse = jnp.where(lane < width, coarse, 0.0)
    projected = residual - along_modes(coarse)
    current = direction = image = dual_direction = share = None
    for iteration in range(ITERS):
        applied = apply_dual(projected)
        pieces = [dot(projected, applied), 0.5 * dot(projected, projected)]
        if iteration:
            pieces += [dot(projected, dual_direction), dot(direction, dual_direction)]
        payload = exact(applied, spread, NT)
        for place, piece in enumerate(pieces):
            payload = jnp.where(lane == width + place, piece, payload)
        paired, sums = talk(3 + iteration, applied, payload)
        added = jnp.where(lane < width, sums, 0.0)
        curved = sums[:, width : width + 1]
        following = sums[:, width + 1 : width + 2]
        if iteration:
            beta = following / current
            curved = curved + beta * (2.0 * sums[:, width + 2 : width + 3] + beta * sums[:, width + 3 : width + 4])
            direction = projected + beta * direction
            image = paired + beta * image
            share = added + beta * share
            dual_direction = applied + beta * dual_direction
        else:
            direction, image, share, dual_direction = projected, paired, added, applied
        current = following
        alpha = current / curved
        multipliers = multipliers + alpha * direction
        residual = residual - alpha * image
        coarse = coarse - alpha * share
        projected = residual - along_modes(coarse)
    mult_out[...] = multipliers
    proj_out[...] = projected
    for copy in started:
        copy.wait_send()


def iterate(clusters, subs, width, solved, half, coarse_load, select):
    loads = coarse_load.shape[0]
    slots = solved.shape[1]
    turns = 3 + ITERS
    vmem = pl.BlockSpec(memory_space=pltpu.VMEM)
    shape = jax.ShapeDtypeStruct((loads, slots), F32)
    return pl.pallas_call(
        functools.partial(cg_kernel, clusters, subs, width),
        out_shape=(shape, shape),
        in_specs=[vmem] * 4,
        out_specs=(vmem, vmem),
        scratch_shapes=[
            pltpu.VMEM((turns, subs + 1, loads + 8, EDGE), F32),
            pltpu.VMEM((turns, subs + 1, loads + 8, EDGE), F32),
            pltpu.VMEM((turns, 8, EDGE), F32),
            pltpu.VMEM((turns, clusters - 1, 8, EDGE), F32),
            pltpu.VMEM((slots, slots), BF),
            pltpu.VMEM((slots, slots), BF),
            pltpu.SemaphoreType.DMA((turns, subs + 1)),
            pltpu.SemaphoreType.DMA((turns, subs + 1)),
            pltpu.SemaphoreType.DMA((turns, clusters - 1)),
            pltpu.SemaphoreType.DMA((turns, clusters - 1)),
        ],
        compiler_params=pltpu.CompilerParams(
            collective_id=0, has_side_effects=True, vmem_limit_bytes=48 * 1024 * 1024
        ),
    )(solved, half, coarse_load, select)


def local(factor_tiles, rigid_modes, load_cases, coarse_load, peer_slots, slot_unknown):
    sub_count = lax.axis_size("sub")
    cluster_count = lax.axis_size("cluster")
    cluster_index = lax.axis_index("cluster")
    within = lax.axis_index("sub")
    own_index = cluster_index * sub_count + within
    table = peer_slots[0]
    devices, most = table.shape
    slots = slot_unknown.shape[1]
    mode_count = rigid_modes.shape[1]
    width = coarse_load.shape[0]
    loads = load_cases.shape[1]

    steps = jnp.arange(1, sub_count, dtype=jnp.int32)
    peers = jnp.concatenate(
        [
            cluster_index * sub_count + (within + steps) % sub_count,
            (own_index - sub_count)[None],
            (own_index + sub_count)[None],
        ]
    )
    there = (peers >= 0) & (peers < devices)
    lists = jnp.where(there[:, None], table[jnp.clip(peers, 0, devices - 1)], slots)
    lists = jnp.pad(lists, ((0, 0), (0, EDGE - most)), constant_values=slots)
    upward = jnp.where(peers > own_index, 1.0, -1.0).astype(F32)
    hits = jnp.arange(slots, dtype=jnp.int32)[:, None] == lists.reshape(-1)[None, :]
    signs = jnp.sum(jnp.where(hits, jnp.repeat(upward, EDGE)[None, :], 0.0), axis=1, keepdims=True)
    select = hits.astype(BF)

    rigid = jnp.pad(rigid_modes[0], ((0, 8 - mode_count), (0, 0)))
    solved, thirds_of = solve(factor_tiles[0], slot_unknown[0][:, None], signs, load_cases[0], rigid)
    half = thirds_of[:mode_count] + thirds_of[8 : 8 + mode_count] + thirds_of[16 : 16 + mode_count]
    member = (jnp.arange(cluster_count, dtype=jnp.int32) == cluster_index).astype(F32)
    half = (half[None] * member[:, None, None]).reshape(width, slots)
    half = jnp.pad(half, ((0, loads - width), (0, 0)))
    begin = jnp.pad(coarse_load.T, ((0, 0), (0, EDGE - width)))
    multipliers, projected = iterate(cluster_count, sub_count, width, solved, half, begin, select)
    return (multipliers.T[None], projected.T[None])


def solution(mesh):
    return jax.shard_map(
        local,
        mesh=mesh,
        in_specs=(
            P(("cluster", "sub"), None, None, None),
            P(("cluster", "sub"), None, None),
            P(("cluster", "sub"), None, None),
            P(),
            P(("cluster", "sub"), None, None),
            P(("cluster", "sub"), None),
        ),
        out_specs=(P(("cluster", "sub"), None, None), P(("cluster", "sub"), None, None)),
        check_vma=False,
    )
```

```python
import functools

import jax
import jax.numpy as jnp
from jax import lax
from jax.experimental import pallas as pl
from jax.experimental.pallas import tpu as pltpu
from jax.sharding import PartitionSpec as P

ITERS = 2
HIGH = lax.Precision.HIGHEST
BF = jnp.bfloat16
F32 = jnp.float32
EDGE = 128
BLOCK = 256
SMALL = 32
NN = (((1,), (0,)), ((), ()))
NT = (((1,), (1,)), ((), ()))


def split(value):
    high = value.astype(BF)
    return high, (value - high.astype(F32)).astype(BF)


def mul(left, right, dims):
    return lax.dot_general(left, right, dims, preferred_element_type=F32)


def mul3(left, right, dims):
    (along,), (across,) = dims[0]
    wide = jnp.concatenate([left[0], left[1], left[0]], axis=along)
    return mul(wide, jnp.concatenate([right[0], right[0], right[1]], axis=across), dims)


def exact(left, right, dims):
    return lax.dot_general(left, right, dims, precision=HIGH, preferred_element_type=F32)


def thirds(value):
    high = value.astype(BF).astype(F32)
    rest = value - high
    middle = rest.astype(BF).astype(F32)
    return jnp.concatenate([high, middle, rest - middle], axis=0).astype(BF)


def picked_by(value, ones, dims):
    rows = value.shape[0]
    parts = mul(thirds(value), ones, dims)
    return parts[:rows] + parts[rows : 2 * rows] + parts[2 * rows :]


def invert_tiles(tiles):
    count = len(tiles)
    lane = lax.broadcasted_iota(jnp.int32, (SMALL, EDGE), 1)
    row = lax.broadcasted_iota(jnp.int32, (SMALL, EDGE), 0)
    packed = []
    for tile in tiles:
        total = jnp.zeros((SMALL, EDGE), F32)
        for b in range(EDGE // SMALL):
            total = jnp.where(lane // SMALL == b, tile[b * SMALL : (b + 1) * SMALL], total)
        packed.append(total)
    solved = [jnp.where(lane % SMALL == row, 1.0, 0.0).astype(F32)] * count
    base = lane // SMALL * SMALL
    for k in range(SMALL):
        for t in range(count):
            column = jnp.take_along_axis(packed[t], base + k, axis=1)
            pivot_row = solved[t][k : k + 1] / column[k : k + 1]
            lowered = solved[t] - jnp.where(row > k, column, 0.0) * pivot_row
            solved[t] = jnp.where(row == k, pivot_row, lowered)
    full_row = lax.broadcasted_iota(jnp.int32, (EDGE, EDGE), 0)
    full_col = lax.broadcasted_iota(jnp.int32, (EDGE, EDGE), 1)
    results = []
    for t in range(count):
        results.append(
            jnp.concatenate(
                [jnp.where(lane // SMALL == b, solved[t], 0.0) for b in range(EDGE // SMALL)],
                axis=0,
            )
        )
    size = SMALL
    while size < EDGE:
        below = (full_row // size == full_col // size + 1) & (full_row // size % 2 == 1)
        for t in range(count):
            corner = split(jnp.where(below, tiles[t], 0.0))
            parts = split(results[t])
            first = split(mul3(parts, corner, NN))
            results[t] = results[t] - mul3(first, parts, NN)
        size *= 2
    return results


def solve_kernel(
    blocks, slots, packed, nodes, signs, loads, rigid, out, modes,
    tiles, corners, inv_hi, inv_lo, y_hi, y_lo, acc, all_sem, corner_sem,
):
    def tile_at(i, j):
        return i * (i + 1) // 2 + j

    group = 4

    def corner_copies(i):
        first = pltpu.make_async_copy(
            packed.at[pl.ds(tile_at(2 * i, 2 * i), 1)], corners.at[i, pl.ds(0, 1)], corner_sem.at[i, 0]
        )
        second = pltpu.make_async_copy(
            packed.at[pl.ds(tile_at(2 * i + 1, 2 * i), 2)], corners.at[i, pl.ds(1, 2)], corner_sem.at[i, 1]
        )
        return first, second

    for i in range(blocks):
        for copy in corner_copies(i):
            copy.start()
    whole_copy = pltpu.make_async_copy(packed, tiles, all_sem)
    whole_copy.start()
    out[...] = jnp.zeros_like(out)
    modes[...] = jnp.zeros_like(modes)
    for i in range(blocks):
        for copy in corner_copies(i):
            copy.wait()

    def invert(step, carry):
        picks = [step * group + g for g in range(group)]
        diagonals = []
        for i in picks:
            diagonals.append(corners[i, 0])
            diagonals.append(corners[i, 2])
        inverses = invert_tiles(diagonals)
        for g, i in enumerate(picks):
            upper, lower = inverses[2 * g], inverses[2 * g + 1]
            corner = split(corners[i, 1])
            below = -mul3(split(mul3(split(lower), corner, NN)), split(upper), NN)
            whole = jnp.concatenate(
                [
                    jnp.concatenate([upper, jnp.zeros((EDGE, EDGE), F32)], axis=1),
                    jnp.concatenate([below, lower], axis=1),
                ],
                axis=0,
            )
            inv_hi[i], inv_lo[i] = split(whole)
        return carry

    lax.fori_loop(0, blocks // group, invert, 0)
    whole_copy.wait()

    def block_row(i, carry):
        columns = pl.ds(pl.multiple_of(i * BLOCK, BLOCK), BLOCK)
        place = i * BLOCK + lax.broadcasted_iota(jnp.int32, (slots, BLOCK), 1)
        gluing = jnp.where(place == nodes[...], signs[...], 0.0)
        modes[...] += mul(thirds(rigid[:, columns]), gluing.astype(BF), NT)
        acc[:slots] = gluing
        acc[slots:] = loads[:, columns]

        def subtract(j, inner):
            above, under = tile_at(2 * i, 2 * j), tile_at(2 * i + 1, 2 * j)
            block = jnp.concatenate(
                [
                    jnp.concatenate([tiles[above], tiles[above + 1]], axis=1),
                    jnp.concatenate([tiles[under], tiles[under + 1]], axis=1),
                ],
                axis=0,
            )
            acc[...] -= mul3((y_hi[j], y_lo[j]), split(block), NT)
            return inner

        lax.fori_loop(0, i, subtract, 0)
        y = split(mul3(split(acc[...]), (inv_hi[i], inv_lo[i]), NT))
        y_hi[i], y_lo[i] = y
        out[...] += mul3(y, (y[0][:slots], y[1][:slots]), NT)
        return carry

    lax.fori_loop(0, blocks, block_row, 0)


def solve(tiles, nodes, signs, loads, rigid):
    slots = nodes.shape[0]
    unknowns = loads.shape[1]
    wide = slots + loads.shape[0]
    blocks = unknowns // BLOCK
    vmem = pl.BlockSpec(memory_space=pltpu.VMEM)
    return pl.pallas_call(
        functools.partial(solve_kernel, blocks, slots),
        out_shape=(
            jax.ShapeDtypeStruct((wide, slots), F32),
            jax.ShapeDtypeStruct((3 * rigid.shape[0], slots), F32),
        ),
        in_specs=[pl.BlockSpec(memory_space=pl.ANY)] + [vmem] * 4,
        out_specs=(vmem, vmem),
        scratch_shapes=[
            pltpu.VMEM(tiles.shape, F32),
            pltpu.VMEM((blocks, 3, EDGE, EDGE), F32),
            pltpu.VMEM((blocks, BLOCK, BLOCK), BF),
            pltpu.VMEM((blocks, BLOCK, BLOCK), BF),
            pltpu.VMEM((blocks, wide, BLOCK), BF),
            pltpu.VMEM((blocks, wide, BLOCK), BF),
            pltpu.VMEM((wide, BLOCK), F32),
            pltpu.SemaphoreType.DMA,
            pltpu.SemaphoreType.DMA((blocks, 2)),
        ],
        compiler_params=pltpu.CompilerParams(vmem_limit_bytes=56 * 1024 * 1024),
    )(tiles, nodes, signs, loads, rigid)


def cg_kernel(
    clusters, subs, width, solved, half, coarse_load, select, mult_out, proj_out,
    send, recv, cross_send, cross_recv, dual_hi, dual_lo, send_sem, recv_sem, cross_send_sem, cross_recv_sem,
):
    loads, slots = mult_out.shape
    cluster = lax.axis_index("cluster")
    sub = lax.axis_index("sub")
    inner = subs - 1
    blocks = inner + 2
    lower, upper = inner, inner + 1
    started = []
    lane = lax.broadcasted_iota(jnp.int32, (loads, EDGE), 1)

    recv[0, lower] = jnp.zeros(recv.shape[2:], F32)
    recv[0, upper] = jnp.zeros(recv.shape[2:], F32)
    for turn in range(2, 2 + 1 + ITERS):
        recv[turn, lower] = jnp.zeros(recv.shape[2:], F32)
        recv[turn, upper] = jnp.zeros(recv.shape[2:], F32)

    barrier = pltpu.get_barrier_semaphore()
    for step in range(1, subs):
        pl.semaphore_signal(
            barrier, inc=1, device_id=(cluster, lax.rem(sub + step, subs)), device_id_type=pl.DeviceIdType.MESH
        )
    for step in range(1, clusters):
        pl.semaphore_signal(
            barrier, inc=1, device_id=(lax.rem(cluster + step, clusters), sub), device_id_type=pl.DeviceIdType.MESH
        )
    pl.semaphore_wait(barrier, subs - 1 + clusters - 1)

    def to_neighbour(turn, source, target, device):
        return pltpu.make_async_remote_copy(
            src_ref=send.at[turn, source, pl.ds(0, loads)],
            dst_ref=recv.at[turn, target, pl.ds(0, loads)],
            send_sem=send_sem.at[turn, source],
            recv_sem=recv_sem.at[turn, target],
            device_id=(device, sub),
            device_id_type=pl.DeviceIdType.MESH,
        )

    def talk(turn, values, payload):
        first = 0 if values is not None else loads
        last = loads + 8 if payload is not None else loads
        if values is not None:
            chosen = picked_by(values, select[...], NN)
            for b in range(blocks):
                send[turn, b, :loads] = chosen[:, b * EDGE : (b + 1) * EDGE]
        if payload is not None:
            compact = payload[:8]
            for part in range(1, loads // 8):
                compact = compact + pltpu.roll(payload[8 * part : 8 * part + 8], 32 * part, 1)
            for b in range(inner):
                send[turn, b, loads:] = compact
        copies = []
        for step in range(1, subs):
            copies.append(
                pltpu.make_async_remote_copy(
                    src_ref=send.at[turn, step - 1, pl.ds(first, last - first)],
                    dst_ref=recv.at[turn, subs - step - 1, pl.ds(first, last - first)],
                    send_sem=send_sem.at[turn, step - 1],
                    recv_sem=recv_sem.at[turn, subs - step - 1],
                    device_id=(cluster, lax.rem(sub + step, subs)),
                    device_id_type=pl.DeviceIdType.MESH,
                )
            )
            copies[-1].start()
        if values is not None:
            down = to_neighbour(turn, lower, upper, lax.rem(cluster + clusters - 1, clusters))
            up = to_neighbour(turn, upper, lower, lax.rem(cluster + 1, clusters))

            @pl.when(cluster > 0)
            def _():
                down.start()

            @pl.when(cluster < clusters - 1)
            def _():
                up.start()

        for copy in copies:
            copy.wait_recv()
        started.extend(copies)
        total = paired = None
        across = []
        if payload is not None:
            total = compact
            for b in range(inner):
                total = total + recv[turn, b, loads:]
            cross_send[turn] = total
            for step in range(1, clusters):
                across.append(
                    pltpu.make_async_remote_copy(
                        src_ref=cross_send.at[turn],
                        dst_ref=cross_recv.at[turn, clusters - step - 1],
                        send_sem=cross_send_sem.at[turn, step - 1],
                        recv_sem=cross_recv_sem.at[turn, clusters - step - 1],
                        device_id=(lax.rem(cluster + step, clusters), sub),
                        device_id_type=pl.DeviceIdType.MESH,
                    )
                )
                across[-1].start()
        if values is not None:

            @pl.when(cluster > 0)
            def _():
                up.wait_recv()
                down.wait_send()

            @pl.when(cluster < clusters - 1)
            def _():
                down.wait_recv()
                up.wait_send()

            received = jnp.concatenate([recv[turn, b, :loads] for b in range(blocks)], axis=1)
            paired = values + picked_by(received, select[...], NT)
        if payload is not None:
            for copy in across:
                copy.wait_recv()
            started.extend(across)
            for b in range(clusters - 1):
                total = total + cross_recv[turn, b]
            rows = [total] + [pltpu.roll(total, EDGE - 32 * part, 1) for part in range(1, loads // 8)]
            total = jnp.where(lane < 32, jnp.concatenate(rows, axis=0), 0.0)
        return paired, total

    modes, _ = talk(0, half[...], None)
    spread = jnp.concatenate([modes, jnp.zeros((EDGE - loads, slots), F32)], axis=0)
    _, gram = talk(1, None, 0.5 * exact(modes, spread, NT))
    row = lax.broadcasted_iota(jnp.int32, (loads, EDGE), 0)
    inverse = jnp.where(row == lane, 1.0, 0.0).astype(F32)
    for k in range(width):
        scale = 1.0 / jnp.sqrt(gram[k : k + 1, k : k + 1])
        gram_row = gram[k : k + 1] * scale
        inverse_row = inverse[k : k + 1] * scale
        factor = jnp.where(row[:, :1] > k, gram[:, k : k + 1] * scale, 0.0)
        gram = gram - factor * gram_row
        inverse = jnp.where(row == k, inverse_row, inverse - factor * inverse_row)

    def along_modes(values):
        weights = exact(exact(values, inverse, NT), inverse, NN)
        return exact(weights, spread, NN)

    dual_hi[...], dual_lo[...] = split(solved[:slots])

    def apply_dual(values):
        high = values.astype(BF).astype(F32)
        stacked = jnp.concatenate([high, values - high], axis=0).astype(BF)
        product = mul(stacked, dual_lo[...], NT) + mul(stacked, dual_hi[...], NT)
        return product[:loads] + product[loads:]

    def dot(left, right):
        return jnp.sum(left * right, axis=1, keepdims=True)

    multipliers = along_modes(coarse_load[...])
    value = solved[slots:] - apply_dual(multipliers)
    residual, coarse = talk(2, value, exact(value, spread, NT))
    coarse = jnp.where(lane < width, coarse, 0.0)
    projected = residual - along_modes(coarse)
    current = direction = image = dual_direction = share = None
    for iteration in range(ITERS):
        applied = apply_dual(projected)
        pieces = [dot(projected, applied), 0.5 * dot(projected, projected)]
        if iteration:
            pieces += [dot(projected, dual_direction), dot(direction, dual_direction)]
        payload = exact(applied, spread, NT)
        for place, piece in enumerate(pieces):
            payload = jnp.where(lane == width + place, piece, payload)
        paired, sums = talk(3 + iteration, applied, payload)
        added = jnp.where(lane < width, sums, 0.0)
        curved = sums[:, width : width + 1]
        following = sums[:, width + 1 : width + 2]
        if iteration:
            beta = following / current
            curved = curved + beta * (2.0 * sums[:, width + 2 : width + 3] + beta * sums[:, width + 3 : width + 4])
            direction = projected + beta * direction
            image = paired + beta * image
            share = added + beta * share
            dual_direction = applied + beta * dual_direction
        else:
            direction, image, share, dual_direction = projected, paired, added, applied
        current = following
        alpha = current / curved
        multipliers = multipliers + alpha * direction
        residual = residual - alpha * image
        coarse = coarse - alpha * share
        projected = residual - along_modes(coarse)
    mult_out[...] = multipliers
    proj_out[...] = projected
    for copy in started:
        copy.wait_send()


def iterate(clusters, subs, width, solved, half, coarse_load, select):
    loads = coarse_load.shape[0]
    slots = solved.shape[1]
    turns = 3 + ITERS
    vmem = pl.BlockSpec(memory_space=pltpu.VMEM)
    shape = jax.ShapeDtypeStruct((loads, slots), F32)
    return pl.pallas_call(
        functools.partial(cg_kernel, clusters, subs, width),
        out_shape=(shape, shape),
        in_specs=[vmem] * 4,
        out_specs=(vmem, vmem),
        scratch_shapes=[
            pltpu.VMEM((turns, subs + 1, loads + 8, EDGE), F32),
            pltpu.VMEM((turns, subs + 1, loads + 8, EDGE), F32),
            pltpu.VMEM((turns, 8, EDGE), F32),
            pltpu.VMEM((turns, clusters - 1, 8, EDGE), F32),
            pltpu.VMEM((slots, slots), BF),
            pltpu.VMEM((slots, slots), BF),
            pltpu.SemaphoreType.DMA((turns, subs + 1)),
            pltpu.SemaphoreType.DMA((turns, subs + 1)),
            pltpu.SemaphoreType.DMA((turns, clusters - 1)),
            pltpu.SemaphoreType.DMA((turns, clusters - 1)),
        ],
        compiler_params=pltpu.CompilerParams(
            collective_id=0, has_side_effects=True, vmem_limit_bytes=48 * 1024 * 1024
        ),
    )(solved, half, coarse_load, select)


def local(factor_tiles, rigid_modes, load_cases, coarse_load, peer_slots, slot_unknown):
    sub_count = lax.axis_size("sub")
    cluster_count = lax.axis_size("cluster")
    cluster_index = lax.axis_index("cluster")
    within = lax.axis_index("sub")
    own_index = cluster_index * sub_count + within
    table = peer_slots[0]
    devices, most = table.shape
    slots = slot_unknown.shape[1]
    mode_count = rigid_modes.shape[1]
    width = coarse_load.shape[0]
    loads = load_cases.shape[1]

    steps = jnp.arange(1, sub_count, dtype=jnp.int32)
    peers = jnp.concatenate(
        [
            cluster_index * sub_count + (within + steps) % sub_count,
            (own_index - sub_count)[None],
            (own_index + sub_count)[None],
        ]
    )
    there = (peers >= 0) & (peers < devices)
    lists = jnp.where(there[:, None], table[jnp.clip(peers, 0, devices - 1)], slots)
    lists = jnp.pad(lists, ((0, 0), (0, EDGE - most)), constant_values=slots)
    upward = jnp.where(peers > own_index, 1.0, -1.0).astype(F32)
    hits = jnp.arange(slots, dtype=jnp.int32)[:, None] == lists.reshape(-1)[None, :]
    signs = jnp.sum(jnp.where(hits, jnp.repeat(upward, EDGE)[None, :], 0.0), axis=1, keepdims=True)
    select = hits.astype(BF)

    rigid = jnp.pad(rigid_modes[0], ((0, 8 - mode_count), (0, 0)))
    solved, thirds_of = solve(factor_tiles[0], slot_unknown[0][:, None], signs, load_cases[0], rigid)
    half = thirds_of[:mode_count] + thirds_of[8 : 8 + mode_count] + thirds_of[16 : 16 + mode_count]
    member = (jnp.arange(cluster_count, dtype=jnp.int32) == cluster_index).astype(F32)
    half = (half[None] * member[:, None, None]).reshape(width, slots)
    half = jnp.pad(half, ((0, loads - width), (0, 0)))
    begin = jnp.pad(coarse_load.T, ((0, 0), (0, EDGE - width)))
    multipliers, projected = iterate(cluster_count, sub_count, width, solved, half, begin, select)
    return (multipliers.T[None], projected.T[None])


def solution(mesh):
    return jax.shard_map(
        local,
        mesh=mesh,
        in_specs=(
            P(("cluster", "sub"), None, None, None),
            P(("cluster", "sub"), None, None),
            P(("cluster", "sub"), None, None),
            P(),
            P(("cluster", "sub"), None, None),
            P(("cluster", "sub"), None),
        ),
        out_specs=(P(("cluster", "sub"), None, None), P(("cluster", "sub"), None, None)),
        check_vma=False,
    )
```
